32 devices in a mesh: frames: 2 (over core), phon: 4 (over y, x), chap: 4 (over z).
Axes of the slice: x: 2, y: 2, z: 4, core: 2. Of those that a mesh axis runs over, the one named last changes fastest.
Arguments:
- queries: bfloat16 [4096, 512], P(('chap', 'frames')), parts along dimension 0, may hold values from -80 to 80
- keys: bfloat16 [16384, 512], P(('chap', 'phon', 'frames')), parts along dimension 0, may hold values from -7 to 7
- values: bfloat16 [16384, 512], P(('chap', 'phon', 'frames')), parts along dimension 0, may hold values from -6 to 6
- band_first: int32 [8], P(('chap', 'frames')), parts along dimension 0, may hold values from 0 to 6, as said below
- cotangent: bfloat16 [4096, 512], P(('chap', 'frames')), parts along dimension 0, may hold values from -6 to 6
Outputs:
- aligned: bfloat16 [4096, 512], P(('chap', 'frames')), parts along dimension 0
- grad_query: bfloat16 [4096, 512], P(('chap', 'frames')), parts along dimension 0
- grad_key: float32 [16384, 512], P(('chap', 'phon', 'frames')), parts along dimension 0
- grad_value: float32 [16384, 512], P(('chap', 'phon', 'frames')), parts along dimension 0
The draws below stay inside these ranges and needn't reach their ends.
There are 4 independent parts, one for each index of `chap`. The reference program is written for one: setup_inputs(seed, part) draws one part's arguments, and reference() takes and returns one part's arrays. A program takes and returns all parts, laid end to end along the dimension named above; each array names one. Nothing has to cross between parts.
Inputs may be any that keep to these rules, and one draw needn't show every extreme that they name: Query tile i attends the key tiles band_first[i] to band_first[i] + 1.
All inputs are finite; a program needn't handle non-finite values.
Results may differ from the reference program's by a relative error of at most 0.022.
Values may be sent and summed in bfloat16 or wider, within the bound.
A program may use at most 64 MiB of HBM per device.

```python
import jax
import jax.numpy as jnp
from jax import lax

D = 512
TILE = 512
NBAND = 2
FRAMES = 1024
PHONES = 4096
QT = 2
KT = 8


def band_plan(key):
    inner = jax.random.fold_in(key, 11)
    tiles = jnp.arange(QT, dtype=jnp.int32)
    base = tiles * (KT - NBAND) // (QT - 1)
    jitter = jax.random.randint(inner, (QT,), -1, 2).astype(jnp.int32)
    jitter = jnp.where((tiles == 0) | (tiles == QT - 1), 0, jitter)
    return jnp.clip(base + jitter, 0, KT - NBAND).astype(jnp.int32)


def key_table(key):
    inner = jax.random.fold_in(key, 23)
    table = jnp.clip(jax.random.normal(inner, (PHONES, D), jnp.float32), -6.0, 6.0)
    return table


def draw_band_first(key, part):
    return band_plan(key)


def draw_keys(key, part):
    return key_table(key).astype(jnp.bfloat16)


def draw_queries(key, part):
    inner = jax.random.fold_in(key, 41)
    base = jnp.clip(jax.random.normal(inner, (FRAMES, D), jnp.float32), -6.0, 6.0)
    return base.astype(jnp.bfloat16)


def levels(stream_key, shape, shards, smallest, top_value):
    def one(dim, parts):
        draws = jax.random.uniform(jax.random.fold_in(jax.random.fold_in(stream_key, 6), dim), (parts,), jnp.float32, smallest / len(shards), top_value / len(shards))
        return jnp.repeat(jnp.exp(draws), shape[dim] // parts).reshape((-1,) + (1,) * (len(shape) - dim - 1))

    level = one(*shards[0])
    for cut in shards[1:]:
        level = level * one(*cut)
    return level


def centred(stream_key, dims, spread, bound, cuts=(), kind=jnp.bfloat16):
    result = jax.random.normal(stream_key, dims, jnp.float32) * spread
    if len(cuts) > 0:
        result = levels(stream_key, dims, cuts, -0.22, 0.18) * result
    return jnp.clip(result, min=-bound, max=bound).astype(kind)


def setup_inputs(seed: int = 0, part: int = 0) -> dict:
    arg_keys = jax.random.split(jax.random.key(seed), 6)
    part_keys = jax.random.split(jax.random.fold_in(arg_keys[5], part), 6)
    return {
        "queries": draw_queries(jax.random.fold_in(jax.random.fold_in(arg_keys[5], part), 71), part),
        "keys": draw_keys(jax.random.fold_in(jax.random.fold_in(arg_keys[5], part), 71), part),
        "values": centred(part_keys[2], (PHONES, D), 1.0, 6.0, ((0, 8),)),
        "band_first": draw_band_first(jax.random.fold_in(jax.random.fold_in(arg_keys[5], part), 71), part),
        "cotangent": centred(part_keys[4], (FRAMES, D), 1.0, 6.0, ((0, 2),)),
    }


def tile_pass(q_tile, g_tile, first, keys, values):
    start = (first * TILE).astype(jnp.int32)
    k_band = lax.dynamic_slice_in_dim(keys, start, NBAND * TILE, 0)
    v_band = lax.dynamic_slice_in_dim(values, start, NBAND * TILE, 0)
    scale = D ** -0.5
    k_float = k_band.astype(jnp.float32)
    key_sq = jnp.sum(k_float * k_float, axis=1)
    scores = (jnp.dot(q_tile, k_band.T, preferred_element_type=jnp.float32) - 0.5 * key_sq[None, :]) * scale
    row_max = jnp.max(scores, axis=1, keepdims=True)
    expd = jnp.exp(scores - row_max)
    total = jnp.sum(expd, axis=1, keepdims=True)
    aligned_f = jnp.dot(expd.astype(jnp.bfloat16), v_band, preferred_element_type=jnp.float32) / total
    lse = row_max + jnp.log(total)
    probs = jnp.exp(scores - lse)
    d_probs = jnp.dot(g_tile, v_band.T, preferred_element_type=jnp.float32)
    delta = jnp.sum(g_tile.astype(jnp.float32) * aligned_f, axis=1, keepdims=True)
    d_scores = probs * (d_probs - delta)
    ds_low = d_scores.astype(jnp.bfloat16)
    grad_q = jnp.dot(ds_low, k_band, preferred_element_type=jnp.float32) * scale
    grad_k = (jnp.dot(ds_low.T, q_tile, preferred_element_type=jnp.float32) - jnp.sum(d_scores, axis=0)[:, None] * k_float) * scale
    grad_v = jnp.dot(probs.astype(jnp.bfloat16).T, g_tile, preferred_element_type=jnp.float32)
    return aligned_f.astype(jnp.bfloat16), grad_q.astype(jnp.bfloat16), grad_k, grad_v, start


def reference(queries, keys, values, band_first, cotangent):
    q_tiles = queries.reshape(QT, TILE, D)
    g_tiles = cotangent.reshape(QT, TILE, D)

    def step(carry, item):
        acc_key, acc_value = carry
        q_tile, g_tile, first = item
        out, grad_q, grad_k, grad_v, start = tile_pass(q_tile, g_tile, first, keys, values)
        old_key = lax.dynamic_slice_in_dim(acc_key, start, NBAND * TILE, 0)
        old_value = lax.dynamic_slice_in_dim(acc_value, start, NBAND * TILE, 0)
        acc_key = lax.dynamic_update_slice_in_dim(acc_key, old_key + grad_k, start, 0)
        acc_value = lax.dynamic_update_slice_in_dim(acc_value, old_value + grad_v, start, 0)
        return (acc_key, acc_value), (out, grad_q)

    init = (jnp.zeros((PHONES, D), jnp.float32), jnp.zeros((PHONES, D), jnp.float32))
    (grad_key, grad_value), (outs, grads) = lax.scan(step, init, (q_tiles, g_tiles, band_first))
    return outs.reshape(FRAMES, D), grads.reshape(FRAMES, D), grad_key, grad_value
```

```python
import functools

import jax
import jax.numpy as jnp
from jax import lax
from jax.experimental import pallas as pl
from jax.experimental.pallas import tpu as pltpu
from jax.sharding import PartitionSpec as P

TILE = 512
NBAND = 2
NEG_FILL = -1e30
STEP = 256

F32 = jnp.float32
BF16 = jnp.bfloat16


def dot(a, b, ca, cb):
    return lax.dot_general(a, b, (((ca,), (cb,)), ((), ())), preferred_element_type=F32)


def kernel(
    nf, nphon,
    band, q_hbm, k_hbm, v_hbm, g_hbm,
    al_out, gq_out, gk_out, gv_out,
    q, g, k, v, s, dp, prob, ds, o_part, gq_part, gk_part, gv_part,
    stat, stat_in, o_in, gq_in, gk_in, gv_in,
    local_sem, k_send, k_recv, v_send, v_recv, st_send, st_recv,
    o_send, o_recv, oa_send, oa_recv, q_send, q_recv, qa_send, qa_recv,
    gk_send, gk_recv, gv_send, gv_recv,
):
    f = lax.axis_index("frames")
    p = lax.axis_index("phon")
    nq, width = q.shape
    rows = k_hbm.shape[0]
    block = nf * rows
    part = nq // nphon
    scale = width ** (-0.5)

    def fdev(d):
        return {"frames": lax.rem(f + d + nf, nf)}

    def pdev(d):
        return {"phon": lax.rem(p + d, nphon)}

    def remote(src, dst, send, recv, dev):
        return pltpu.make_async_remote_copy(
            src_ref=src, dst_ref=dst, send_sem=send, recv_sem=recv,
            device_id=dev, device_id_type=pl.DeviceIdType.MESH,
        )

    loads = [
        pltpu.make_async_copy(k_hbm, k.at[pl.ds(0, rows)], local_sem.at[0]),
        pltpu.make_async_copy(q_hbm, q, local_sem.at[1]),
        pltpu.make_async_copy(v_hbm, v.at[pl.ds(0, rows)], local_sem.at[2]),
        pltpu.make_async_copy(g_hbm, g, local_sem.at[3]),
    ]
    for c in loads:
        c.start()

    barrier = pltpu.get_barrier_semaphore()
    for d in range(1, nf):
        pl.semaphore_signal(barrier, inc=1, device_id=fdev(d), device_id_type=pl.DeviceIdType.MESH)
    for d in range(1, nphon):
        pl.semaphore_signal(barrier, inc=1, device_id=pdev(d), device_id_type=pl.DeviceIdType.MESH)
    pl.semaphore_wait(barrier, nf - 1 + nphon - 1)

    pulls = []
    for d in range(1, nf):
        slot = pl.ds(d * rows, rows)
        pulls.append(remote(k_hbm, k.at[slot], k_send.at[d - 1], k_recv.at[d - 1], fdev(d)))
        pulls.append(remote(v_hbm, v.at[slot], v_send.at[d - 1], v_recv.at[d - 1], fdev(d)))
    for c in pulls:
        c.start()

    lane_tile = lax.broadcasted_iota(jnp.int32, (1, nq), 1) // TILE
    first = jnp.zeros((1, nq), jnp.int32)
    for i in range(band.shape[0]):
        first = jnp.where(lane_tile == i, band[i], first)
    ones = jnp.ones((8, width), BF16)

    def scores(t, top):
        r = pl.ds(pl.multiple_of(t * STEP, STEP), STEP)
        kt = k[r, :]
        row = t * STEP + lax.broadcasted_iota(jnp.int32, (STEP, 1), 0)
        src = lax.rem(f - row // rows + nf, nf)
        tile = (p * block + src * rows + lax.rem(row, rows)) // TILE
        kf = kt.astype(F32)
        sq = jnp.sum(kf * kf, axis=1, keepdims=True)
        raw = (dot(kt, q[...], 1, 1) - 0.5 * sq) * scale
        st = jnp.where((tile >= first) & (tile < first + NBAND), raw, NEG_FILL)
        s[r, :] = st
        dp[r, :] = dot(v[r, :], g[...], 1, 1)
        return jnp.maximum(top, jnp.max(st.reshape(STEP // 8, 8, nq), axis=0))

    top = jnp.full((8, nq), NEG_FILL, F32)
    near = rows // STEP if rows % STEP == 0 else 0
    for c in loads:
        c.wait()
    top = lax.fori_loop(0, near, scores, top)
    for c in pulls:
        c.wait_recv()
    top = lax.fori_loop(near, block // STEP, scores, top)
    top = jnp.max(top, axis=0, keepdims=True)

    def expand(t, carry):
        tot, mix = carry
        r = pl.ds(pl.multiple_of(t * STEP, STEP), STEP)
        e = jnp.exp(s[r, :] - top)
        s[r, :] = e
        tot = tot + jnp.sum(e.reshape(STEP // 8, 8, nq), axis=0)
        mix = mix + jnp.sum((e * dp[r, :]).reshape(STEP // 8, 8, nq), axis=0)
        return tot, mix

    zero = jnp.zeros((8, nq), F32)
    tot, mix = lax.fori_loop(0, block // STEP, expand, (zero, zero))
    tot = jnp.sum(tot, axis=0, keepdims=True)
    mix = jnp.sum(mix, axis=0, keepdims=True)
    stat[0:1, :] = top
    stat[1:2, :] = tot
    stat[2:3, :] = mix
    stat[3:8, :] = jnp.zeros((5, nq), F32)
    stats = [
        remote(stat, stat_in.at[d - 1], st_send.at[d - 1], st_recv.at[d - 1], pdev(d))
        for d in range(1, nphon)
    ]
    for c in stats:
        c.start()
    for c in stats:
        c.wait_recv()
    all_top = top
    for d in range(1, nphon):
        all_top = jnp.maximum(all_top, stat_in[d - 1, 0:1, :])
    mine = jnp.exp(top - all_top)
    total = tot * mine
    delta = mix * mine
    for d in range(1, nphon):
        w = jnp.exp(stat_in[d - 1, 0:1, :] - all_top)
        total = total + stat_in[d - 1, 1:2, :] * w
        delta = delta + stat_in[d - 1, 2:3, :] * w
    delta = delta / total
    mine = mine / total

    def soften(t, carry):
        r = pl.ds(pl.multiple_of(t * STEP, STEP), STEP)
        pt = s[r, :] * mine
        prob[r, :] = pt.astype(BF16)
        d_s = pt * (dp[r, :] - delta)
        dp[r, :] = d_s
        ds[r, :] = d_s.astype(BF16)
        return carry

    lax.fori_loop(0, block // STEP, soften, 0)

    def sends(part_ref, in_ref, send, recv):
        out = []
        for d in range(1, nphon):
            j = lax.rem(p + d, nphon)
            r = pl.ds(pl.multiple_of(j * part, part), part)
            out.append(remote(part_ref.at[r], in_ref.at[d - 1], send.at[d - 1], recv.at[d - 1], pdev(d)))
        return out

    o_part[...] = dot(prob[...], v[...], 0, 0).astype(BF16)
    o_rs = sends(o_part, o_in, o_send, o_recv)
    for c in o_rs:
        c.start()
    gq_part[...] = (dot(ds[...], k[...], 0, 0) * scale).astype(BF16)
    q_rs = sends(gq_part, gq_in, q_send, q_recv)
    for c in q_rs:
        c.start()

    def key_grads(t, carry):
        t = lax.rem(t + near, block // STEP)
        r = pl.ds(pl.multiple_of(t * STEP, STEP), STEP)
        col = jnp.sum(dp[r, :], axis=1, keepdims=True)
        gk = (dot(ds[r, :], q[...], 1, 0) - col * k[r, :].astype(F32)) * scale
        gk_part[r, :] = gk.astype(BF16)
        gv_part[r, :] = dot(prob[r, :], g[...], 1, 0).astype(BF16)
        return carry

    far = block // STEP - near
    lax.fori_loop(0, far, key_grads, 0)
    back = []
    for d in range(1, nf):
        slot = pl.ds(d * rows, rows)
        back.append(remote(gk_part.at[slot], gk_in.at[d - 1], gk_send.at[d - 1], gk_recv.at[d - 1], fdev(-d)))
        back.append(remote(gv_part.at[slot], gv_in.at[d - 1], gv_send.at[d - 1], gv_recv.at[d - 1], fdev(-d)))
    for c in back:
        c.start()
    lax.fori_loop(far, block // STEP, key_grads, 0)

    own = pl.ds(pl.multiple_of(p * part, part), part)

    def spread(rs, part_ref, in_ref, out_ref, send, recv):
        for c in rs:
            c.wait_recv()
        acc = part_ref[own, :].astype(F32)
        for d in range(1, nphon):
            acc = acc + in_ref[d - 1].astype(F32)
        out_ref[own, :] = acc.astype(BF16)
        ag = [
            remote(out_ref.at[own], out_ref.at[own], send.at[d - 1], recv.at[d - 1], pdev(d))
            for d in range(1, nphon)
        ]
        for c in ag:
            c.start()
        return ag

    o_ag = spread(o_rs, o_part, o_in, al_out, oa_send, oa_recv)
    q_ag = spread(q_rs, gq_part, gq_in, gq_out, qa_send, qa_recv)

    for c in back:
        c.wait_recv()
    gk = gk_part[pl.ds(0, rows), :].astype(F32)
    gv = gv_part[pl.ds(0, rows), :].astype(F32)
    for d in range(1, nf):
        gk = gk + gk_in[d - 1].astype(F32)
        gv = gv + gv_in[d - 1].astype(F32)
    gk_out[...] = gk
    gv_out[...] = gv

    for c in o_ag + q_ag:
        c.wait_recv()
    for c in pulls + stats + o_rs + q_rs + back + o_ag + q_ag:
        c.wait_send()


def body(nf, nphon, queries, keys, values, band_first, cotangent):
    nq, width = queries.shape
    rows = keys.shape[0]
    block = rows * nf
    part = nq // nphon
    hbm = pl.BlockSpec(memory_space=pl.ANY)
    vmem = pl.BlockSpec(memory_space=pltpu.VMEM)
    dma = pltpu.SemaphoreType.DMA
    return pl.pallas_call(
        functools.partial(kernel, nf, nphon),
        out_shape=(
            jax.ShapeDtypeStruct((nq, width), BF16),
            jax.ShapeDtypeStruct((nq, width), BF16),
            jax.ShapeDtypeStruct((rows, width), F32),
            jax.ShapeDtypeStruct((rows, width), F32),
        ),
        in_specs=[pl.BlockSpec(memory_space=pltpu.SMEM), hbm, hbm, hbm, hbm],
        out_specs=(vmem,) * 4,
        scratch_shapes=[
            pltpu.VMEM((nq, width), BF16),
            pltpu.VMEM((nq, width), BF16),
            pltpu.VMEM((block, width), BF16),
            pltpu.VMEM((block, width), BF16),
            pltpu.VMEM((block, nq), F32),
            pltpu.VMEM((block, nq), F32),
            pltpu.VMEM((block, nq), BF16),
            pltpu.VMEM((block, nq), BF16),
            pltpu.VMEM((nq, width), BF16),
            pltpu.VMEM((nq, width), BF16),
            pltpu.VMEM((block, width), BF16),
            pltpu.VMEM((block, width), BF16),
            pltpu.VMEM((8, nq), F32),
            pltpu.VMEM((nphon - 1, 8, nq), F32),
            pltpu.VMEM((nphon - 1, part, width), BF16),
            pltpu.VMEM((nphon - 1, part, width), BF16),
            pltpu.VMEM((nf - 1, rows, width), BF16),
            pltpu.VMEM((nf - 1, rows, width), BF16),
            dma((4,)),
        ]
        + [dma((nf - 1,))] * 4
        + [dma((nphon - 1,))] * 10
        + [dma((nf - 1,))] * 4,
        compiler_params=pltpu.CompilerParams(
            collective_id=0, has_side_effects=True, vmem_limit_bytes=48 * 2**20
        ),
    )(band_first, queries, keys, values, cotangent)


def solution(mesh):
    tile = P(("chap", "frames"), None)
    key = P(("chap", "phon", "frames"), None)
    return jax.shard_map(
        functools.partial(body, mesh.shape["frames"], mesh.shape["phon"]),
        mesh=mesh,
        in_specs=(tile, key, key, P(("chap", "frames")), tile),
        out_specs=(tile, tile, key, key),
        check_vma=False,
    )
```

```python
import functools

import jax
import jax.numpy as jnp
from jax import lax
from jax.experimental import pallas as pl
from jax.experimental.pallas import tpu as pltpu
from jax.sharding import PartitionSpec as P

TILE = 512
NBAND = 2
NEG_FILL = -1e30
STEP = 256

F32 = jnp.float32
BF16 = jnp.bfloat16


def dot(a, b, ca, cb):
    return lax.dot_general(a, b, (((ca,), (cb,)), ((), ())), preferred_element_type=F32)


def kernel(
    nf, nphon,
    band, q_hbm, k_hbm, v_hbm, g_hbm,
    al_hbm, gq_hbm, gk_hbm, gv_hbm,
    al_out, gq_out, gk_out, gv_out,
    q, g, k, v, s, dp, prob, ds, o_part, gq_part, gk_part, gv_part,
    stat, stat_in, o_in1, o_sum, o_in2, q_in1, q_sum, q_in2, gk_in, gv_in,
    local_sem, store_sem, k_send, k_recv, v_send, v_recv, st_send, st_recv,
    o_send, o_recv, q_send, q_recv,
    gk_send, gk_recv, gv_send, gv_recv,
):
    f = lax.axis_index("frames")
    p = lax.axis_index("phon")
    nq, width = q.shape
    rows = k_hbm.shape[0]
    block = nf * rows
    scale = width ** (-0.5)

    def fdev(d):
        return {"frames": lax.rem(f + d + nf, nf)}

    def pdev(d):
        return {"phon": lax.rem(p + d, nphon)}

    def remote(src, dst, send, recv, dev):
        return pltpu.make_async_remote_copy(
            src_ref=src, dst_ref=dst, send_sem=send, recv_sem=recv,
            device_id=dev, device_id_type=pl.DeviceIdType.MESH,
        )

    loads = [
        pltpu.make_async_copy(k_hbm, k.at[pl.ds(0, rows)], local_sem.at[0]),
        pltpu.make_async_copy(q_hbm, q, local_sem.at[1]),
        pltpu.make_async_copy(v_hbm, v.at[pl.ds(0, rows)], local_sem.at[2]),
        pltpu.make_async_copy(g_hbm, g, local_sem.at[3]),
    ]
    for c in loads:
        c.start()

    barrier = pltpu.get_barrier_semaphore()
    for d in range(1, nf):
        pl.semaphore_signal(barrier, inc=1, device_id=fdev(d), device_id_type=pl.DeviceIdType.MESH)
    for d in range(1, nphon):
        pl.semaphore_signal(barrier, inc=1, device_id=pdev(d), device_id_type=pl.DeviceIdType.MESH)
    pl.semaphore_wait(barrier, nf - 1 + nphon - 1)

    pulls = []
    for d in range(1, nf):
        slot = pl.ds(d * rows, rows)
        pulls.append(remote(k_hbm, k.at[slot], k_send.at[d - 1], k_recv.at[d - 1], fdev(d)))
        pulls.append(remote(v_hbm, v.at[slot], v_send.at[d - 1], v_recv.at[d - 1], fdev(d)))
    for c in pulls:
        c.start()

    lane_tile = lax.broadcasted_iota(jnp.int32, (1, nq), 1) // TILE
    first = jnp.zeros((1, nq), jnp.int32)
    for i in range(band.shape[0]):
        first = jnp.where(lane_tile == i, band[i], first)
    ones = jnp.ones((8, width), BF16)

    def scores(t, top):
        r = pl.ds(pl.multiple_of(t * STEP, STEP), STEP)
        kt = k[r, :]
        row = t * STEP + lax.broadcasted_iota(jnp.int32, (STEP, 1), 0)
        src = lax.rem(f - row // rows + nf, nf)
        tile = (p * block + src * rows + lax.rem(row, rows)) // TILE
        kf = kt.astype(F32)
        sq = jnp.sum(kf * kf, axis=1, keepdims=True)
        raw = (dot(kt, q[...], 1, 1) - 0.5 * sq) * scale
        st = jnp.where((tile >= first) & (tile < first + NBAND), raw, NEG_FILL)
        s[r, :] = st
        dp[r, :] = dot(v[r, :], g[...], 1, 1)
        return jnp.maximum(top, jnp.max(st.reshape(STEP // 8, 8, nq), axis=0))

    top = jnp.full((8, nq), NEG_FILL, F32)
    near = rows // STEP if rows % STEP == 0 else 0
    for c in loads:
        c.wait()
    top = lax.fori_loop(0, near, scores, top)
    for c in pulls:
        c.wait_recv()
    top = lax.fori_loop(near, block // STEP, scores, top)
    top = jnp.max(top, axis=0, keepdims=True)

    def expand(t, carry):
        tot, mix = carry
        r = pl.ds(pl.multiple_of(t * STEP, STEP), STEP)
        e = jnp.exp(s[r, :] - top)
        s[r, :] = e
        tot = tot + jnp.sum(e.reshape(STEP // 8, 8, nq), axis=0)
        mix = mix + jnp.sum((e * dp[r, :]).reshape(STEP // 8, 8, nq), axis=0)
        return tot, mix

    zero = jnp.zeros((8, nq), F32)
    tot, mix = lax.fori_loop(0, block // STEP, expand, (zero, zero))
    tot = jnp.sum(tot, axis=0, keepdims=True)
    mix = jnp.sum(mix, axis=0, keepdims=True)
    stat[0:1, :] = top
    stat[1:2, :] = tot
    stat[2:3, :] = mix
    stat[3:8, :] = jnp.zeros((5, nq), F32)
    stats = [
        remote(stat, stat_in.at[d - 1], st_send.at[d - 1], st_recv.at[d - 1], pdev(d))
        for d in range(1, nphon)
    ]
    for c in stats:
        c.start()
    for c in stats:
        c.wait_recv()
    all_top = top
    for d in range(1, nphon):
        all_top = jnp.maximum(all_top, stat_in[d - 1, 0:1, :])
    mine = jnp.exp(top - all_top)
    total = tot * mine
    delta = mix * mine
    for d in range(1, nphon):
        w = jnp.exp(stat_in[d - 1, 0:1, :] - all_top)
        total = total + stat_in[d - 1, 1:2, :] * w
        delta = delta + stat_in[d - 1, 2:3, :] * w
    delta = delta / total
    mine = mine / total

    def soften(t, carry):
        r = pl.ds(pl.multiple_of(t * STEP, STEP), STEP)
        pt = s[r, :] * mine
        prob[r, :] = pt.astype(BF16)
        d_s = pt * (dp[r, :] - delta)
        dp[r, :] = d_s
        ds[r, :] = d_s.astype(BF16)
        return carry

    lax.fori_loop(0, block // STEP, soften, 0)

    x, y = lax.rem(p, 2), p // 2
    xdev = {"phon": y * 2 + 1 - x}
    ydev = {"phon": (1 - y) * 2 + x}
    half, quarter, eighth = nq // 2, nq // 4, nq // 8

    def at(offset, size, unit):
        return pl.ds(pl.multiple_of(offset, unit), size)

    def first_step(part_ref, in1, send, recv):
        copies = [
            remote(part_ref.at[at((1 - x) * quarter, quarter, quarter)], in1.at[0], send.at[0], recv.at[0], xdev),
            remote(part_ref.at[at(half + (1 - y) * quarter, quarter, quarter)], in1.at[1], send.at[1], recv.at[1], ydev),
        ]
        for c in copies:
            c.start()
        return copies

    def second_step(copies, part_ref, in1, sum1, in2, send, recv):
        out = []
        for i, (base, near_bit, far_dev) in enumerate(((x * quarter, y, ydev), (half + y * quarter, x, xdev))):
            copies[i].wait_recv()
            both = part_ref[at(base, quarter, quarter), :].astype(F32) + in1[i].astype(F32)
            sum1[i] = both.astype(BF16)
            c = remote(
                sum1.at[i, at((1 - near_bit) * eighth, eighth, eighth)], in2.at[i],
                send.at[2 + i], recv.at[2 + i], far_dev,
            )
            c.start()
            out.append(c)
        return out

    def rows_of(px, py):
        return (
            at(px * quarter + py * eighth, eighth, eighth),
            at(half + py * quarter + px * eighth, eighth, eighth),
        )

    def third_step(copies, sum1, in2, out_ref, send, recv):
        mine_rows = rows_of(x, y)
        out = []
        for i, near_bit in enumerate((y, x)):
            copies[i].wait_recv()
            total_rows = sum1[i, at(near_bit * eighth, eighth, eighth), :].astype(F32) + in2[i].astype(F32)
            out_ref[mine_rows[i], :] = total_rows.astype(BF16)
            view = out_ref.at[mine_rows[i]]
            for j, dev in enumerate((xdev, ydev)):
                n = 4 + 2 * i + j
                c = remote(view, view, send.at[n], recv.at[n], dev)
                c.start()
                out.append(c)
        return out

    def fourth_step(copies, out_ref, send, recv):
        out = []
        copies[1].wait_recv()
        view = out_ref.at[rows_of(x, 1 - y)[0]]
        out.append(remote(view, view, send.at[8], recv.at[8], xdev))
        out[0].start()
        copies[2].wait_recv()
        view = out_ref.at[rows_of(1 - x, y)[1]]
        out.append(remote(view, view, send.at[9], recv.at[9], ydev))
        out[1].start()
        return out

    o_part[...] = dot(prob[...], v[...], 0, 0).astype(BF16)
    o_1 = first_step(o_part, o_in1, o_send, o_recv)
    gq_part[...] = (dot(ds[...], k[...], 0, 0) * scale).astype(BF16)
    q_1 = first_step(gq_part, q_in1, q_send, q_recv)
    o_2 = second_step(o_1, o_part, o_in1, o_sum, o_in2, o_send, o_recv)

    def key_grads(t, carry):
        t = lax.rem(t + near, block // STEP)
        r = pl.ds(pl.multiple_of(t * STEP, STEP), STEP)
        col = jnp.sum(dp[r, :], axis=1, keepdims=True)
        gk = (dot(ds[r, :], q[...], 1, 0) - col * k[r, :].astype(F32)) * scale
        gk_part[r, :] = gk.astype(BF16)
        gv_part[r, :] = dot(prob[r, :], g[...], 1, 0).astype(BF16)
        return carry

    far = block // STEP - near
    lax.fori_loop(0, far, key_grads, 0)
    back = []
    for d in range(1, nf):
        slot = pl.ds(d * rows, rows)
        back.append(remote(gk_part.at[slot], gk_in.at[d - 1], gk_send.at[d - 1], gk_recv.at[d - 1], fdev(-d)))
        back.append(remote(gv_part.at[slot], gv_in.at[d - 1], gv_send.at[d - 1], gv_recv.at[d - 1], fdev(-d)))
    for c in back:
        c.start()
    lax.fori_loop(far, block // STEP, key_grads, 0)

    q_2 = second_step(q_1, gq_part, q_in1, q_sum, q_in2, q_send, q_recv)
    o_3 = third_step(o_2, o_sum, o_in2, al_out, o_send, o_recv)
    q_3 = third_step(q_2, q_sum, q_in2, gq_out, q_send, q_recv)
    o_4 = fourth_step(o_3, al_out, o_send, o_recv)

    for c in back:
        c.wait_recv()
    gk = gk_part[pl.ds(0, rows), :].astype(F32)
    gv = gv_part[pl.ds(0, rows), :].astype(F32)
    for d in range(1, nf):
        gk = gk + gk_in[d - 1].astype(F32)
        gv = gv + gv_in[d - 1].astype(F32)
    gk_out[...] = gk
    gv_out[...] = gv
    stores = [
        pltpu.make_async_copy(gk_out, gk_hbm, store_sem.at[0]),
        pltpu.make_async_copy(gv_out, gv_hbm, store_sem.at[1]),
        pltpu.make_async_copy(al_out, al_hbm, store_sem.at[2]),
        pltpu.make_async_copy(gq_out, gq_hbm, store_sem.at[3]),
    ]
    stores[0].start()
    stores[1].start()

    q_4 = fourth_step(q_3, gq_out, q_send, q_recv)
    for copies, last, out in ((o_3, o_4, stores[2]), (q_3, q_4, stores[3])):
        copies[0].wait_recv()
        copies[3].wait_recv()
        for c in last:
            c.wait_recv()
        out.start()
    for c in pulls + stats + back + o_1 + o_2 + o_3 + o_4 + q_1 + q_2 + q_3 + q_4:
        c.wait_send()
    for c in stores:
        c.wait()


def store(*refs):
    n = len(refs) // 2
    copies = [pltpu.make_async_copy(refs[i], refs[n + i], refs[-1].at[i]) for i in range(n)]
    for c in copies:
        c.start()
    for c in copies:
        c.wait()


def body(nf, nphon, queries, keys, values, band_first, cotangent):
    nq, width = queries.shape
    rows = keys.shape[0]
    block = rows * nf
    hbm = pl.BlockSpec(memory_space=pl.ANY)
    dma = pltpu.SemaphoreType.DMA
    results = pl.pallas_call(
        functools.partial(kernel, nf, nphon),
        out_shape=(
            jax.ShapeDtypeStruct((nq, width), BF16),
            jax.ShapeDtypeStruct((nq, width), BF16),
            jax.ShapeDtypeStruct((rows, width), F32),
            jax.ShapeDtypeStruct((rows, width), F32),
        ),
        in_specs=[pl.BlockSpec(memory_space=pltpu.SMEM), hbm, hbm, hbm, hbm],
        out_specs=(hbm,) * 4,
        scratch_shapes=[
            pltpu.VMEM((nq, width), BF16),
            pltpu.VMEM((nq, width), BF16),
            pltpu.VMEM((rows, width), F32),
            pltpu.VMEM((rows, width), F32),
            pltpu.VMEM((nq, width), BF16),
            pltpu.VMEM((nq, width), BF16),
            pltpu.VMEM((block, width), BF16),
            pltpu.VMEM((block, width), BF16),
            pltpu.VMEM((block, nq), F32),
            pltpu.VMEM((block, nq), F32),
            pltpu.VMEM((block, nq), BF16),
            pltpu.VMEM((block, nq), BF16),
            pltpu.VMEM((nq, width), BF16),
            pltpu.VMEM((nq, width), BF16),
            pltpu.VMEM((block, width), BF16),
            pltpu.VMEM((block, width), BF16),
            pltpu.VMEM((8, nq), F32),
            pltpu.VMEM((nphon - 1, 8, nq), F32),
        ]
        + [
            pltpu.VMEM((2, nq // 4, width), BF16),
            pltpu.VMEM((2, nq // 4, width), BF16),
            pltpu.VMEM((2, nq // 8, width), BF16),
        ] * 2
        + [
            pltpu.VMEM((nf - 1, rows, width), BF16),
            pltpu.VMEM((nf - 1, rows, width), BF16),
            dma((4,)),
            dma((4,)),
        ]
        + [dma((nf - 1,))] * 4
        + [dma((nphon - 1,))] * 2
        + [dma((10,))] * 4
        + [dma((nf - 1,))] * 4,
        compiler_params=pltpu.CompilerParams(
            collective_id=0, has_side_effects=True, vmem_limit_bytes=60 * 2**20
        ),
    )(band_first, queries, keys, values, cotangent)
    return pl.pallas_call(
        store,
        out_shape=tuple(jax.ShapeDtypeStruct(r.shape, r.dtype) for r in results),
        in_specs=[hbm] * 4,
        out_specs=(hbm,) * 4,
        scratch_shapes=[dma((4,))],
    )(*results)


def solution(mesh):
    tile = P(("chap", "frames"), None)
    key = P(("chap", "phon", "frames"), None)
    return jax.shard_map(
        functools.partial(body, mesh.shape["frames"], mesh.shape["phon"]),
        mesh=mesh,
        in_specs=(tile, key, key, P(("chap", "frames")), tile),
        out_specs=(tile, tile, key, key),
        check_vma=False,
    )
```

```python
import functools

import jax
import jax.numpy as jnp
from jax import lax
from jax.experimental import pallas as pl
from jax.experimental.pallas import tpu as pltpu
from jax.sharding import PartitionSpec as P

TILE = 512
NBAND = 2
NEG_FILL = -1e30
STEP = 256

F32 = jnp.float32
BF16 = jnp.bfloat16


def dot(a, b, ca, cb):
    return lax.dot_general(a, b, (((ca,), (cb,)), ((), ())), preferred_element_type=F32)


def kernel(
    nf, nphon,
    band, q_hbm, k_hbm, v_hbm, g_hbm,
    al_hbm, gq_hbm, gk_hbm, gv_hbm,
    al_out, gq_out, gk_out, gv_out,
    q, g, k, v, o_raw, s, dp, prob, ds, o_part, gq_part, gk_part, gv_part,
    stat, stat_in, o_in1, o_sum, o_in2, q_in1, q_sum, q_in2, gk_in, gv_in,
    local_sem, store_sem, k_send, k_recv, v_send, v_recv, st_send, st_recv,
    o_send, o_recv, q_send, q_recv,
    gk_send, gk_recv, gv_send, gv_recv,
):
    f = lax.axis_index("frames")
    p = lax.axis_index("phon")
    nq, width = q.shape
    rows = k_hbm.shape[0]
    block = nf * rows
    scale = width ** (-0.5)

    def fdev(d):
        return {"frames": lax.rem(f + d + nf, nf)}

    def pdev(d):
        return {"phon": lax.rem(p + d, nphon)}

    def remote(src, dst, send, recv, dev):
        return pltpu.make_async_remote_copy(
            src_ref=src, dst_ref=dst, send_sem=send, recv_sem=recv,
            device_id=dev, device_id_type=pl.DeviceIdType.MESH,
        )

    loads = [
        pltpu.make_async_copy(k_hbm, k.at[pl.ds(0, rows)], local_sem.at[0]),
        pltpu.make_async_copy(q_hbm, q, local_sem.at[1]),
        pltpu.make_async_copy(v_hbm, v.at[pl.ds(0, rows)], local_sem.at[2]),
        pltpu.make_async_copy(g_hbm, g, local_sem.at[3]),
    ]
    for c in loads:
        c.start()

    barrier = pltpu.get_barrier_semaphore()
    for d in range(1, nf):
        pl.semaphore_signal(barrier, inc=1, device_id=fdev(d), device_id_type=pl.DeviceIdType.MESH)
    for d in range(1, nphon):
        pl.semaphore_signal(barrier, inc=1, device_id=pdev(d), device_id_type=pl.DeviceIdType.MESH)
    pl.semaphore_wait(barrier, nf - 1 + nphon - 1)

    pulls = []
    for d in range(1, nf):
        slot = pl.ds(d * rows, rows)
        pulls.append(remote(k_hbm, k.at[slot], k_send.at[d - 1], k_recv.at[d - 1], fdev(d)))
        pulls.append(remote(v_hbm, v.at[slot], v_send.at[d - 1], v_recv.at[d - 1], fdev(d)))
    for c in pulls:
        c.start()

    lane_tile = lax.broadcasted_iota(jnp.int32, (1, nq), 1) // TILE
    first = jnp.zeros((1, nq), jnp.int32)
    for i in range(band.shape[0]):
        first = jnp.where(lane_tile == i, band[i], first)

    def scores(t, top):
        r = pl.ds(pl.multiple_of(t * STEP, STEP), STEP)
        kt = k[r, :]
        row = t * STEP + lax.broadcasted_iota(jnp.int32, (STEP, 1), 0)
        src = lax.rem(f - row // rows + nf, nf)
        tile = (p * block + src * rows + lax.rem(row, rows)) // TILE
        kf = kt.astype(F32)
        sq = jnp.sum(kf * kf, axis=1, keepdims=True)
        raw = (dot(kt, q[...], 1, 1) - 0.5 * sq) * scale
        st = jnp.where((tile >= first) & (tile < first + NBAND), raw, NEG_FILL)
        s[r, :] = st
        dp[r, :] = dot(v[r, :], g[...], 1, 1)
        return jnp.maximum(top, jnp.max(st.reshape(STEP // 8, 8, nq), axis=0))

    top = jnp.full((8, nq), NEG_FILL, F32)
    near = rows // STEP if rows % STEP == 0 else 0
    for c in loads:
        c.wait()
    top = lax.fori_loop(0, near, scores, top)
    for c in pulls:
        c.wait_recv()
    top = lax.fori_loop(near, block // STEP, scores, top)
    top = jnp.max(top, axis=0, keepdims=True)

    def expand(t, carry):
        tot, mix = carry
        r = pl.ds(pl.multiple_of(t * STEP, STEP), STEP)
        e = jnp.exp(s[r, :] - top)
        s[r, :] = e
        prob[r, :] = e.astype(BF16)
        tot = tot + jnp.sum(e.reshape(STEP // 8, 8, nq), axis=0)
        mix = mix + jnp.sum((e * dp[r, :]).reshape(STEP // 8, 8, nq), axis=0)
        return tot, mix

    zero = jnp.zeros((8, nq), F32)
    tot, mix = lax.fori_loop(0, block // STEP, expand, (zero, zero))
    tot = jnp.sum(tot, axis=0, keepdims=True)
    mix = jnp.sum(mix, axis=0, keepdims=True)
    stat[0:1, :] = top
    stat[1:2, :] = tot
    stat[2:3, :] = mix
    stat[3:8, :] = jnp.zeros((5, nq), F32)
    stats = [
        remote(stat, stat_in.at[d - 1], st_send.at[d - 1], st_recv.at[d - 1], pdev(d))
        for d in range(1, nphon)
    ]
    for c in stats:
        c.start()
    o_raw[...] = dot(prob[...], v[...], 0, 0)
    for c in stats:
        c.wait_recv()
    all_top = top
    for d in range(1, nphon):
        all_top = jnp.maximum(all_top, stat_in[d - 1, 0:1, :])
    mine = jnp.exp(top - all_top)
    total = tot * mine
    delta = mix * mine
    for d in range(1, nphon):
        w = jnp.exp(stat_in[d - 1, 0:1, :] - all_top)
        total = total + stat_in[d - 1, 1:2, :] * w
        delta = delta + stat_in[d - 1, 2:3, :] * w
    delta = delta / total
    mine = mine / total
    column = jnp.swapaxes(jnp.broadcast_to(mine, (8, nq)), 0, 1)[:, 0:1]
    o_part[...] = (o_raw[...] * column).astype(BF16)

    x, y = lax.rem(p, 2), p // 2
    xdev = {"phon": y * 2 + 1 - x}
    ydev = {"phon": (1 - y) * 2 + x}
    half, quarter, eighth = nq // 2, nq // 4, nq // 8

    def at(offset, size, unit):
        return pl.ds(pl.multiple_of(offset, unit), size)

    def first_step(part_ref, in1, send, recv):
        copies = [
            remote(part_ref.at[at((1 - x) * quarter, quarter, quarter)], in1.at[0], send.at[0], recv.at[0], xdev),
            remote(part_ref.at[at(half + (1 - y) * quarter, quarter, quarter)], in1.at[1], send.at[1], recv.at[1], ydev),
        ]
        for c in copies:
            c.start()
        return copies

    def second_step(copies, part_ref, in1, sum1, in2, send, recv):
        out = []
        for i, (base, near_bit, far_dev) in enumerate(((x * quarter, y, ydev), (half + y * quarter, x, xdev))):
            copies[i].wait_recv()
            both = part_ref[at(base, quarter, quarter), :].astype(F32) + in1[i].astype(F32)
            sum1[i] = both.astype(BF16)
            c = remote(
                sum1.at[i, at((1 - near_bit) * eighth, eighth, eighth)], in2.at[i],
                send.at[2 + i], recv.at[2 + i], far_dev,
            )
            c.start()
            out.append(c)
        return out

    def rows_of(px, py):
        return (
            at(px * quarter + py * eighth, eighth, eighth),
            at(half + py * quarter + px * eighth, eighth, eighth),
        )

    def third_step(copies, sum1, in2, out_ref, send, recv):
        mine_rows = rows_of(x, y)
        out = []
        for i, near_bit in enumerate((y, x)):
            copies[i].wait_recv()
            total_rows = sum1[i, at(near_bit * eighth, eighth, eighth), :].astype(F32) + in2[i].astype(F32)
            out_ref[mine_rows[i], :] = total_rows.astype(BF16)
            view = out_ref.at[mine_rows[i]]
            for j, dev in enumerate((xdev, ydev)):
                n = 4 + 2 * i + j
                c = remote(view, view, send.at[n], recv.at[n], dev)
                c.start()
                out.append(c)
        return out

    def fourth_step(copies, out_ref, send, recv):
        out = []
        copies[1].wait_recv()
        view = out_ref.at[rows_of(x, 1 - y)[0]]
        out.append(remote(view, view, send.at[8], recv.at[8], xdev))
        out[0].start()
        copies[2].wait_recv()
        view = out_ref.at[rows_of(1 - x, y)[1]]
        out.append(remote(view, view, send.at[9], recv.at[9], ydev))
        out[1].start()
        return out

    o_1 = first_step(o_part, o_in1, o_send, o_recv)

    def soften(t, carry):
        r = pl.ds(pl.multiple_of(t * STEP, STEP), STEP)
        pt = s[r, :] * mine
        prob[r, :] = pt.astype(BF16)
        d_s = pt * (dp[r, :] - delta)
        dp[r, :] = d_s
        ds[r, :] = d_s.astype(BF16)
        return carry

    lax.fori_loop(0, block // STEP, soften, 0)

    gq_part[...] = (dot(ds[...], k[...], 0, 0) * scale).astype(BF16)
    q_1 = first_step(gq_part, q_in1, q_send, q_recv)

    def key_grads(t, carry):
        t = lax.rem(t + near, block // STEP)
        r = pl.ds(pl.multiple_of(t * STEP, STEP), STEP)
        col = jnp.sum(dp[r, :], axis=1, keepdims=True)
        gk = (dot(ds[r, :], q[...], 1, 0) - col * k[r, :].astype(F32)) * scale
        gk_part[r, :] = gk.astype(BF16)
        gv_part[r, :] = dot(prob[r, :], g[...], 1, 0).astype(BF16)
        return carry

    far = block // STEP - near
    lax.fori_loop(0, far, key_grads, 0)
    back = []
    for d in range(1, nf):
        slot = pl.ds(d * rows, rows)
        back.append(remote(gk_part.at[slot], gk_in.at[d - 1], gk_send.at[d - 1], gk_recv.at[d - 1], fdev(-d)))
        back.append(remote(gv_part.at[slot], gv_in.at[d - 1], gv_send.at[d - 1], gv_recv.at[d - 1], fdev(-d)))
    for c in back:
        c.start()
    o_2 = second_step(o_1, o_part, o_in1, o_sum, o_in2, o_send, o_recv)
    lax.fori_loop(far, block // STEP, key_grads, 0)

    q_2 = second_step(q_1, gq_part, q_in1, q_sum, q_in2, q_send, q_recv)
    o_3 = third_step(o_2, o_sum, o_in2, al_out, o_send, o_recv)
    q_3 = third_step(q_2, q_sum, q_in2, gq_out, q_send, q_recv)
    o_4 = fourth_step(o_3, al_out, o_send, o_recv)

    for c in back:
        c.wait_recv()
    gk = gk_part[pl.ds(0, rows), :].astype(F32)
    gv = gv_part[pl.ds(0, rows), :].astype(F32)
    for d in range(1, nf):
        gk = gk + gk_in[d - 1].astype(F32)
        gv = gv + gv_in[d - 1].astype(F32)
    gk_out[...] = gk
    gv_out[...] = gv
    stores = [
        pltpu.make_async_copy(gk_out, gk_hbm, store_sem.at[0]),
        pltpu.make_async_copy(gv_out, gv_hbm, store_sem.at[1]),
        pltpu.make_async_copy(al_out, al_hbm, store_sem.at[2]),
        pltpu.make_async_copy(gq_out, gq_hbm, store_sem.at[3]),
    ]
    stores[0].start()
    stores[1].start()

    q_4 = fourth_step(q_3, gq_out, q_send, q_recv)
    for copies, last, out in ((o_3, o_4, stores[2]), (q_3, q_4, stores[3])):
        copies[0].wait_recv()
        copies[3].wait_recv()
        for c in last:
            c.wait_recv()
        out.start()
    for c in pulls + stats + back + o_1 + o_2 + o_3 + o_4 + q_1 + q_2 + q_3 + q_4:
        c.wait_send()
    for c in stores:
        c.wait()


def store(*refs):
    n = (len(refs) - 2) // 3
    srcs, dsts, bufs, (load_sem, store_sem) = refs[:n], refs[n:2 * n], refs[2 * n:3 * n], refs[3 * n:]
    loads = [pltpu.make_async_copy(srcs[i], bufs[i], load_sem.at[i]) for i in range(n)]
    stores = [pltpu.make_async_copy(bufs[i], dsts[i], store_sem.at[i]) for i in range(n)]
    for c in loads:
        c.start()
    for c, d in zip(loads, stores):
        c.wait()
        d.start()
    for c in stores:
        c.wait()


def body(nf, nphon, queries, keys, values, band_first, cotangent):
    nq, width = queries.shape
    rows = keys.shape[0]
    block = rows * nf
    hbm = pl.BlockSpec(memory_space=pl.ANY)
    dma = pltpu.SemaphoreType.DMA
    results = pl.pallas_call(
        functools.partial(kernel, nf, nphon),
        out_shape=(
            jax.ShapeDtypeStruct((nq, width), BF16),
            jax.ShapeDtypeStruct((nq, width), BF16),
            jax.ShapeDtypeStruct((rows, width), F32),
            jax.ShapeDtypeStruct((rows, width), F32),
        ),
        in_specs=[pl.BlockSpec(memory_space=pltpu.SMEM), hbm, hbm, hbm, hbm],
        out_specs=(hbm,) * 4,
        scratch_shapes=[
            pltpu.VMEM((nq, width), BF16),
            pltpu.VMEM((nq, width), BF16),
            pltpu.VMEM((rows, width), F32),
            pltpu.VMEM((rows, width), F32),
            pltpu.VMEM((nq, width), BF16),
            pltpu.VMEM((nq, width), BF16),
            pltpu.VMEM((block, width), BF16),
            pltpu.VMEM((block, width), BF16),
            pltpu.VMEM((nq, width), F32),
            pltpu.VMEM((block, nq), F32),
            pltpu.VMEM((block, nq), F32),
            pltpu.VMEM((block, nq), BF16),
            pltpu.VMEM((block, nq), BF16),
            pltpu.VMEM((nq, width), BF16),
            pltpu.VMEM((nq, width), BF16),
            pltpu.VMEM((block, width), BF16),
            pltpu.VMEM((block, width), BF16),
            pltpu.VMEM((8, nq), F32),
            pltpu.VMEM((nphon - 1, 8, nq), F32),
        ]
        + [
            pltpu.VMEM((2, nq // 4, width), BF16),
            pltpu.VMEM((2, nq // 4, width), BF16),
            pltpu.VMEM((2, nq // 8, width), BF16),
        ] * 2
        + [
            pltpu.VMEM((nf - 1, rows, width), BF16),
            pltpu.VMEM((nf - 1, rows, width), BF16),
            dma((4,)),
            dma((4,)),
        ]
        + [dma((nf - 1,))] * 4
        + [dma((nphon - 1,))] * 2
        + [dma((10,))] * 4
        + [dma((nf - 1,))] * 4,
        compiler_params=pltpu.CompilerParams(
            collective_id=0, has_side_effects=True, vmem_limit_bytes=60 * 2**20
        ),
    )(band_first, queries, keys, values, cotangent)
    return pl.pallas_call(
        store,
        out_shape=tuple(jax.ShapeDtypeStruct(r.shape, r.dtype) for r in results),
        in_specs=[hbm] * 4,
        out_specs=(hbm,) * 4,
        scratch_shapes=[pltpu.VMEM(r.shape, r.dtype) for r in results] + [dma((4,))] * 2,
    )(*results)


def solution(mesh):
    tile = P(("chap", "frames"), None)
    key = P(("chap", "phon", "frames"), None)
    return jax.shard_map(
        functools.partial(body, mesh.shape["frames"], mesh.shape["phon"]),
        mesh=mesh,
        in_specs=(tile, key, key, P(("chap", "frames")), tile),
        out_specs=(tile, tile, key, key),
        check_vma=False,
    )
```
